32 devices in a mesh: grid: 8 (over y, x, core), dom: 4 (over z).
Axes of the slice: x: 2, y: 2, z: 4, core: 2. Of those that a mesh axis runs over, the one named last changes fastest.
Arguments:
- values: float32 [8, 16, 4, 4, 8, 8, 128], P('grid', 'dom'), may hold values from -2 to 2
- levels: int32 [8, 6], P('grid'), may hold values from 0 to 7, as said below
- coefficients: int32 [8], P('grid'), may hold values from -3 to 3, as said below
Outputs:
- combined: float32 [8, 16, 4, 4, 8, 8, 128], P('grid', 'dom')
The draws below stay inside these ranges and needn't reach their ends.
Inputs may be any that keep to these rules, and one draw needn't show every extreme that they name: levels[g, k] is grid g's level along dimension k + 1. With L_k the base-two logarithm of that dimension's extent (16, 4, 4, 8, 8, 128), each entry lies between L_k - 2 and L_k, and the shortfalls L_k - levels[g, k] of one grid add up to 2 at most. `coefficients`: every coefficient is nonzero.
All inputs are finite; a program needn't handle non-finite values.
Results may differ from the reference program's by a relative error of at most 0.0003.
Values sent between devices are 32-bit elements; how exact they have to be, the bound alone decides.
A program may use at most 64 MiB of HBM per device.

```python
import jax
import jax.numpy as jnp
import numpy as np
from jax import lax

EXT_B = 4
EXT_C = 4
EXT_D = 8
EXT_E = 8
EXT_F = 128
EXT_A = 16
GROUPS = 8


def draw_levels(key, part):
    picks = jax.random.randint(jax.random.fold_in(key, 11), (GROUPS, 2), 0, 7)
    doubled = jax.random.randint(jax.random.fold_in(key, 13), (), 0, GROUPS)
    single = jax.random.randint(jax.random.fold_in(key, 17), (), 0, GROUPS)
    picks = picks.at[single, 0].set(0)
    picks = picks.at[doubled].set(0)
    tops = jnp.array([EXT_A.bit_length() - 1, EXT_B.bit_length() - 1, EXT_C.bit_length() - 1, EXT_D.bit_length() - 1, EXT_E.bit_length() - 1, EXT_F.bit_length() - 1], dtype=jnp.int32)
    dims = jnp.arange(0, 6, dtype=jnp.int32)
    shortfall = jnp.sum((picks[:, :, None] == dims[None, None, :]).astype(jnp.int32), axis=1)
    return (tops[None, :] - shortfall).astype(jnp.int32)


def draw_coefficients(key, part):
    magnitude = jax.random.randint(jax.random.fold_in(key, 23), (GROUPS,), 1, 4)
    signs = jax.random.randint(jax.random.fold_in(key, 29), (GROUPS,), 0, 2) * 2 - 1
    return (magnitude * signs).astype(jnp.int32)


def shard_levels(key, shape, pieces, least, largest):
    def one(axis_at, parts):
        draws = jax.random.uniform(jax.random.fold_in(jax.random.fold_in(key, 6), axis_at), (parts,), jnp.float32, least / len(pieces), largest / len(pieces))
        return jnp.repeat(jnp.exp(draws), shape[axis_at] // parts).reshape((-1,) + (1,) * (len(shape) - axis_at - 1))

    gain = one(*pieces[0])
    for cut in pieces[1:]:
        gain = gain * one(*cut)
    return gain


def gaussian(rng, extent, width, bound, pieces=(), kind=jnp.bfloat16):
    drawn = width * jax.random.normal(rng, extent, jnp.float32)
    if pieces:
        drawn = drawn * shard_levels(rng, extent, pieces, -0.22, 0.18)
    return jnp.clip(drawn, -bound, bound).astype(kind)


def setup_inputs(seed: int = 0) -> dict:
    key_list = jax.random.split(jax.random.key(seed), 4)
    return {
        "values": gaussian(key_list[0], (GROUPS, EXT_A, EXT_B, EXT_C, EXT_D, EXT_E, EXT_F), 0.3, 2.0, ((0, 8), (1, 4)), jnp.float32),
        "levels": draw_levels(jax.random.fold_in(key_list[3], 71), 0),
        "coefficients": draw_coefficients(jax.random.fold_in(key_list[3], 71), 0),
    }


PRECISE = lax.Precision.HIGHEST


def coarse_position(numerator, level_now):
    while numerator > 0 and numerator % 2 == 0:
        numerator = numerator // 2
        level_now = level_now - 1
    if numerator == 0:
        return 0
    return (1 << (level_now - 1)) + (numerator - 1) // 2


def parent_positions(position):
    level_now = position.bit_length()
    span_size = 1 << (level_now - 1)
    offset = position - span_size
    return [coarse_position(offset % span_size, level_now - 1), coarse_position((offset + 1) % span_size, level_now - 1)]


def hier_table(points):
    matrix = np.eye(points)
    for position in range(1, points):
        for parent in parent_positions(position):
            matrix[position, parent] -= 0.5
    return matrix


def dehier_table(points):
    matrix = np.zeros((points, points))
    matrix[0, 0] = 1.0
    for position in range(1, points):
        row_now = np.zeros(points)
        row_now[position] = 1.0
        for parent in parent_positions(position):
            row_now = row_now + 0.5 * matrix[parent]
        matrix[position] = row_now
    return matrix


def nodal_order(points):
    placed = np.zeros(points, dtype=np.int64)
    for position in range(1, points):
        level_now = position.bit_length()
        offset = position - (1 << (level_now - 1))
        placed[position] = (2 * offset + 1) * points // (1 << level_now)
    return placed


def nodal_table(matrix):
    placed = nodal_order(matrix.shape[0])
    result = np.zeros(matrix.shape)
    result[placed[:, None], placed[None, :]] = matrix
    return result


def apply_table(grid_data, matrix, dim_index):
    letters = "abcdefg"[:grid_data.ndim]
    outputs = letters[:dim_index] + "z" + letters[dim_index + 1:]
    formula = letters + ",z" + letters[dim_index] + "->" + outputs
    return jnp.einsum(formula, grid_data, jnp.asarray(matrix, dtype=jnp.float32), precision=PRECISE)


def holding_mask(level_row, extents):
    holding = jnp.ones(extents, dtype=jnp.float32)
    for dim_index, points in enumerate(extents):
        count = level_row[dim_index].astype(jnp.int32)
        index = jnp.arange(points, dtype=jnp.int32)
        if dim_index == 0:
            spacing = jnp.right_shift(jnp.int32(points), count)
            inside = (jnp.remainder(index, spacing) == 0).astype(jnp.float32)
        else:
            limit = jnp.left_shift(jnp.int32(1), count)
            inside = (index < limit).astype(jnp.float32)
        shape_now = [1] * len(extents)
        shape_now[dim_index] = points
        holding = holding * inside.reshape(shape_now)
    return holding


def reference(values, levels, coefficients):
    extents = tuple(values.shape[1:])
    forward = [nodal_table(hier_table(values.shape[1]))] + [hier_table(points) for points in extents[1:]]
    backward = [nodal_table(dehier_table(values.shape[1]))] + [dehier_table(points) for points in extents[1:]]

    def accumulate(summed, scan_item):
        grid_data, level_row, weight = scan_item
        for dim_index, matrix in enumerate(forward):
            grid_data = apply_table(grid_data, matrix, dim_index)
        weighted = (weight.astype(jnp.float32) * holding_mask(level_row, extents)) * grid_data
        return summed + weighted, None

    initial = jnp.zeros(extents, dtype=jnp.float32)
    summed, unused = lax.scan(accumulate, initial, (values, levels, coefficients))
    combined = summed
    for dim_index, matrix in enumerate(backward):
        combined = apply_table(combined, matrix, dim_index)

    def restrict(level_row):
        return holding_mask(level_row, extents) * combined

    return lax.map(restrict, levels)
```

```python
import functools

import jax
import jax.numpy as jnp
import numpy as np
from jax import lax
from jax.experimental import pallas as pl
from jax.experimental.pallas import tpu as pltpu
from jax.sharding import PartitionSpec as P

MESH = pl.DeviceIdType.MESH


def coarse_position(numerator, level_now):
    while numerator > 0 and numerator % 2 == 0:
        numerator = numerator // 2
        level_now = level_now - 1
    if numerator == 0:
        return 0
    return (1 << level_now - 1) + (numerator - 1) // 2


def parent_positions(position):
    level_now = position.bit_length()
    span_size = 1 << level_now - 1
    offset = position - span_size
    return [
        coarse_position(offset % span_size, level_now - 1),
        coarse_position((offset + 1) % span_size, level_now - 1),
    ]


def hier_table(points):
    matrix = np.eye(points)
    for position in range(1, points):
        for parent in parent_positions(position):
            matrix[position, parent] -= 0.5
    return matrix


def dehier_table(points):
    matrix = np.zeros((points, points))
    matrix[0, 0] = 1.0
    for position in range(1, points):
        row_now = np.zeros(points)
        row_now[position] = 1.0
        for parent in parent_positions(position):
            row_now = row_now + 0.5 * matrix[parent]
        matrix[position] = row_now
    return matrix


def local_hier(points):
    matrix = np.zeros((points, points + 1))
    matrix[0, 0] = 1.0
    for point in range(1, points):
        stride = point & -point
        matrix[point, point] = 1.0
        matrix[point, point - stride] -= 0.5
        matrix[point, point + stride] -= 0.5
    return matrix


def local_dehier(points):
    matrix = np.zeros((points + 1, points + 1))
    matrix[0, 0] = 1.0
    matrix[points, points] = 1.0
    stride = points // 2
    while stride >= 1:
        for point in range(stride, points, 2 * stride):
            row_now = np.zeros(points + 1)
            row_now[point] = 1.0
            matrix[point] = row_now + 0.5 * (matrix[point - stride] + matrix[point + stride])
        stride = stride // 2
    return matrix[:points]


SHORTFALLS = 3


def projection_tables(points):
    top = points.bit_length() - 1
    hier, dehier = hier_table(points), dehier_table(points)
    return [
        dehier @ np.diag((np.arange(points) < (1 << max(top - s, 0))).astype(np.float64)) @ hier
        for s in range(SHORTFALLS)
    ]


def row_tables(points):
    last = np.zeros((1, points + 1))
    last[0, points] = 1.0
    hier = np.concatenate([local_hier(points), last])
    result = []
    for s in range(SHORTFALLS):
        held = (np.arange(points + 1) % (1 << s) == 0).astype(np.float64)
        held[points] = 1.0
        result.append(local_dehier(points) @ np.diag(held) @ hier)
    return np.stack(result)


def holding_mask(level_row, extents):
    holding = jnp.ones(extents, dtype=jnp.float32)
    for dim_index, points in enumerate(extents):
        limit = jnp.left_shift(jnp.int32(1), level_row[dim_index])
        inside = (jnp.arange(points, dtype=jnp.int32) < limit).astype(jnp.float32)
        shape_now = [1] * len(extents)
        shape_now[dim_index] = points
        holding = holding * inside.reshape(shape_now)
    return holding


def split_rows_mask(level_count, local_rows, rank_count):
    members = lax.axis_size("dom")
    total_rows = local_rows * members
    rows_here = lax.axis_index("dom") * local_rows + jnp.arange(local_rows, dtype=jnp.int32)
    spacing = jnp.right_shift(jnp.int32(total_rows), level_count)
    inside = (jnp.remainder(rows_here, spacing) == 0).astype(jnp.float32)
    return inside.reshape((local_rows,) + (1,) * (rank_count - 1))


def split_dot(data, right=None, left=None):
    high = data.astype(jnp.bfloat16)
    low = (data - high.astype(jnp.float32)).astype(jnp.bfloat16)
    if right is not None:
        return jnp.dot(high, right, preferred_element_type=jnp.float32) + jnp.dot(
            low, right, preferred_element_type=jnp.float32
        )
    return jnp.dot(left, high, preferred_element_type=jnp.float32) + jnp.dot(
        left, low, preferred_element_type=jnp.float32
    )


def kernel(groups, members, v_ref, inner_ref, lane_ref, outer_ref, row_ref, out_ref,
           follow, part, acc, recv, send_sem, recv_sem, z_send, z_recv):
    rows, depth, lanes = v_ref.shape
    steps = groups.bit_length() - 1
    me = lax.axis_index("grid")
    dom = lax.axis_index("dom")
    core = lax.rem(me, 2)
    before = lax.rem(dom + members - 1, members)
    after = lax.rem(dom + 1, members)

    bits, partners = [], []
    for step in range(steps):
        up = 1 << step
        down = 1 << (steps - step) if step else 1
        bit_up = lax.rem(me // up, 2)
        bit_down = lax.rem(me // down, 2)
        bit = bit_up + core * (bit_down - bit_up)
        stride = up + core * (down - up)
        bits.append(bit)
        partners.append(me + (1 - 2 * bit) * stride)

    barrier = pltpu.get_barrier_semaphore()
    for partner in partners:
        pl.semaphore_signal(barrier, inc=1, device_id={"grid": partner}, device_id_type=MESH)
    for near in (before, after):
        pl.semaphore_signal(barrier, inc=1, device_id={"dom": near}, device_id_type=MESH)
    pl.semaphore_wait(barrier, steps + 2)

    shift = pltpu.make_async_remote_copy(
        src_ref=v_ref.at[0], dst_ref=follow, send_sem=z_send, recv_sem=z_recv,
        device_id={"dom": before}, device_id_type=MESH,
    )
    shift.start()

    outer = outer_ref.shape[0]
    span = depth // outer

    def project(data):
        blocks = [split_dot(data[i * span : (i + 1) * span], left=inner_ref[...]) for i in range(outer)]
        mixed = []
        for i in range(outer):
            total = outer_ref[i, 0] * blocks[0]
            for j in range(1, outer):
                total = total + outer_ref[i, j] * blocks[j]
            mixed.append(total)
        return split_dot(jnp.concatenate(mixed, axis=0), right=lane_ref[...])

    def reduce_chunk(index, start, size):
        low, now = start, size
        lows = [low]
        taken = start
        for step in range(steps):
            half = now // 2
            keep = pl.multiple_of(low + bits[step] * half, 8)
            give = pl.multiple_of(low + (1 - bits[step]) * half, 8)
            copy = pltpu.make_async_remote_copy(
                src_ref=acc.at[pl.ds(give, half)], dst_ref=recv.at[pl.ds(taken, half)],
                send_sem=send_sem.at[index, step], recv_sem=recv_sem.at[index, step],
                device_id={"grid": partners[step]}, device_id_type=MESH,
            )
            copy.start()
            yield
            copy.wait()
            total = acc[pl.ds(keep, half), :] + recv[taken : taken + half, :]
            if step == steps - 1:
                out_ref[pl.ds(keep, half), :] = total
            else:
                acc[pl.ds(keep, half), :] = total
            taken += half
            low, now = keep, half
            lows.append(low)
        for step in range(steps - 1, -1, -1):
            mine = out_ref.at[pl.ds(lows[step + 1], now)]
            copy = pltpu.make_async_remote_copy(
                src_ref=mine, dst_ref=mine,
                send_sem=send_sem.at[index, 2 * steps - 1 - step],
                recv_sem=recv_sem.at[index, 2 * steps - 1 - step],
                device_id={"grid": partners[step]}, device_id_type=MESH,
            )
            copy.start()
            yield
            copy.wait()
            now *= 2

    first = project(v_ref[0])
    part[0] = first
    acc[0:depth, :] = row_ref[0, 0] * first
    head = reduce_chunk(0, 0, depth)
    next(head)
    for row in range(1, rows):
        part[row] = project(v_ref[row])
    next(head)
    shift.wait()
    part[rows] = project(follow[...])
    for row in range(1, rows):
        total = row_ref[row, 0] * part[0]
        for source in range(1, rows + 1):
            total = total + row_ref[row, source] * part[source]
        acc[row * depth : (row + 1) * depth, :] = total
    active = [reduce_chunk(1, depth, (rows - 1) * depth), head]
    while active:
        active = [chunk for chunk in active if next(chunk, "end") != "end"]


def body(values, levels, coefficients):
    grid_data = values[0]
    level_row = levels[0]
    weight = coefficients[0].astype(jnp.float32)
    local_rows = grid_data.shape[0]
    extents = tuple(grid_data.shape[1:])
    groups, members = lax.axis_size("grid"), lax.axis_size("dom")
    lanes = extents[-1]
    depth = int(np.prod(extents[:-1]))
    span = depth // extents[0]

    tops = [local_rows * members] + list(extents)
    short = jnp.asarray([t.bit_length() - 1 for t in tops], jnp.int32) - level_row
    third, fourth, fifth = (projection_tables(points) for points in extents[1:4])
    combos = [(i, j, k) for i in range(SHORTFALLS) for j in range(SHORTFALLS) for k in range(SHORTFALLS)
              if i + j + k < SHORTFALLS]
    place = np.zeros((SHORTFALLS,) * 3, np.int32)
    for at, combo in enumerate(combos):
        place[combo] = at
    inner_all = np.stack([np.kron(np.kron(third[i], fourth[j]), fifth[k]) for i, j, k in combos])
    which = jnp.asarray(place)[short[2], short[3], short[4]]
    inner = lax.dynamic_index_in_dim(jnp.asarray(inner_all, jnp.bfloat16), which, 0, keepdims=False)
    lane = lax.dynamic_index_in_dim(
        jnp.asarray(np.stack(projection_tables(lanes)).transpose(0, 2, 1), jnp.bfloat16), short[5], 0, keepdims=False)
    outer = jnp.asarray(np.stack(projection_tables(extents[0])), jnp.float32)[short[1]]
    rows = jnp.asarray(row_tables(local_rows), jnp.float32)[short[0]] * weight

    steps = groups.bit_length() - 1
    vmem = pl.BlockSpec(memory_space=pltpu.VMEM)
    smem = pl.BlockSpec(memory_space=pltpu.SMEM)
    combined = pl.pallas_call(
        functools.partial(kernel, groups, members),
        out_shape=jax.ShapeDtypeStruct((local_rows * depth, lanes), jnp.float32),
        in_specs=[vmem, vmem, vmem, smem, smem],
        out_specs=vmem,
        scratch_shapes=[
            pltpu.VMEM((depth, lanes), jnp.float32),
            pltpu.VMEM((local_rows + 1, depth, lanes), jnp.float32),
            pltpu.VMEM((local_rows * depth, lanes), jnp.float32),
            pltpu.VMEM((local_rows * depth, lanes), jnp.float32),
            pltpu.SemaphoreType.DMA((2, 2 * steps)),
            pltpu.SemaphoreType.DMA((2, 2 * steps)),
            pltpu.SemaphoreType.DMA,
            pltpu.SemaphoreType.DMA,
        ],
        compiler_params=pltpu.CompilerParams(
            collective_id=0, has_side_effects=True, vmem_limit_bytes=40 * 1024 * 1024
        ),
    )(grid_data.reshape(local_rows, depth, lanes), inner, lane, outer, rows)
    holding = (
        split_rows_mask(level_row[0], local_rows, grid_data.ndim)
        * holding_mask(level_row[1:], extents)[None]
    )
    return (holding * combined.reshape(grid_data.shape))[None]


def solution(mesh):
    in_specs = (P("grid", "dom", None, None, None, None, None), P("grid", None), P("grid"))
    out_specs = P("grid", "dom", None, None, None, None, None)
    return jax.shard_map(body, mesh=mesh, in_specs=in_specs, out_specs=out_specs, check_vma=False)
```

```python
import functools

import jax
import jax.numpy as jnp
import numpy as np
from jax import lax
from jax.experimental import pallas as pl
from jax.experimental.pallas import tpu as pltpu
from jax.sharding import PartitionSpec as P

MESH = pl.DeviceIdType.MESH


def coarse_position(numerator, level_now):
    while numerator > 0 and numerator % 2 == 0:
        numerator = numerator // 2
        level_now = level_now - 1
    if numerator == 0:
        return 0
    return (1 << level_now - 1) + (numerator - 1) // 2


def parent_positions(position):
    level_now = position.bit_length()
    span_size = 1 << level_now - 1
    offset = position - span_size
    return [
        coarse_position(offset % span_size, level_now - 1),
        coarse_position((offset + 1) % span_size, level_now - 1),
    ]


def hier_table(points):
    matrix = np.eye(points)
    for position in range(1, points):
        for parent in parent_positions(position):
            matrix[position, parent] -= 0.5
    return matrix


def dehier_table(points):
    matrix = np.zeros((points, points))
    matrix[0, 0] = 1.0
    for position in range(1, points):
        row_now = np.zeros(points)
        row_now[position] = 1.0
        for parent in parent_positions(position):
            row_now = row_now + 0.5 * matrix[parent]
        matrix[position] = row_now
    return matrix


def local_hier(points):
    matrix = np.zeros((points, points + 1))
    matrix[0, 0] = 1.0
    for point in range(1, points):
        stride = point & -point
        matrix[point, point] = 1.0
        matrix[point, point - stride] -= 0.5
        matrix[point, point + stride] -= 0.5
    return matrix


def local_dehier(points):
    matrix = np.zeros((points + 1, points + 1))
    matrix[0, 0] = 1.0
    matrix[points, points] = 1.0
    stride = points // 2
    while stride >= 1:
        for point in range(stride, points, 2 * stride):
            row_now = np.zeros(points + 1)
            row_now[point] = 1.0
            matrix[point] = row_now + 0.5 * (matrix[point - stride] + matrix[point + stride])
        stride = stride // 2
    return matrix[:points]


SHORTFALLS = 3


def projection_tables(points):
    top = points.bit_length() - 1
    hier, dehier = hier_table(points), dehier_table(points)
    return [
        dehier @ np.diag((np.arange(points) < (1 << max(top - s, 0))).astype(np.float64)) @ hier
        for s in range(SHORTFALLS)
    ]


def row_tables(points):
    last = np.zeros((1, points + 1))
    last[0, points] = 1.0
    hier = np.concatenate([local_hier(points), last])
    result = []
    for s in range(SHORTFALLS):
        held = (np.arange(points + 1) % (1 << s) == 0).astype(np.float64)
        held[points] = 1.0
        result.append(local_dehier(points) @ np.diag(held) @ hier)
    return np.stack(result)


def holding_mask(level_row, extents):
    holding = jnp.ones(extents, dtype=jnp.float32)
    for dim_index, points in enumerate(extents):
        limit = jnp.left_shift(jnp.int32(1), level_row[dim_index])
        inside = (jnp.arange(points, dtype=jnp.int32) < limit).astype(jnp.float32)
        shape_now = [1] * len(extents)
        shape_now[dim_index] = points
        holding = holding * inside.reshape(shape_now)
    return holding


def split_rows_mask(level_count, local_rows, rank_count):
    members = lax.axis_size("dom")
    total_rows = local_rows * members
    rows_here = lax.axis_index("dom") * local_rows + jnp.arange(local_rows, dtype=jnp.int32)
    spacing = jnp.right_shift(jnp.int32(total_rows), level_count)
    inside = (jnp.remainder(rows_here, spacing) == 0).astype(jnp.float32)
    return inside.reshape((local_rows,) + (1,) * (rank_count - 1))


def split_dot(data, right=None, left=None):
    high = data.astype(jnp.bfloat16)
    low = (data - high.astype(jnp.float32)).astype(jnp.bfloat16)
    if right is not None:
        return jnp.dot(high, right, preferred_element_type=jnp.float32) + jnp.dot(
            low, right, preferred_element_type=jnp.float32
        )
    return jnp.dot(left, high, preferred_element_type=jnp.float32) + jnp.dot(
        left, low, preferred_element_type=jnp.float32
    )


def pick(tables, short):
    return [
        [jnp.where(short == 0, float(tables[0][i][j]),
                   jnp.where(short == 1, float(tables[1][i][j]), float(tables[2][i][j])))
         for j in range(len(tables[0][0]))]
        for i in range(len(tables[0]))
    ]


def kernel(groups, members, tops, v_ref, level_ref, weight_ref, inner_ref, lane_ref, out_ref,
           follow, part, acc, recv, send_sem, recv_sem, z_send, z_recv):
    rows, depth, lanes = v_ref.shape
    steps = groups.bit_length() - 1
    me = lax.axis_index("grid")
    dom = lax.axis_index("dom")
    core = lax.rem(me, 2)
    before = lax.rem(dom + members - 1, members)
    after = lax.rem(dom + 1, members)

    bits, partners = [], []
    for step in range(steps):
        up = 1 << step
        down = 1 << (steps - step) if step else 1
        bit_up = lax.rem(me // up, 2)
        bit_down = lax.rem(me // down, 2)
        bit = bit_up + core * (bit_down - bit_up)
        stride = up + core * (down - up)
        bits.append(bit)
        partners.append(me + (1 - 2 * bit) * stride)

    short = [
        jnp.clip(top.bit_length() - 1 - level_ref[0, k], 0, SHORTFALLS - 1) for k, top in enumerate(tops)
    ]

    barrier = pltpu.get_barrier_semaphore()
    for partner in partners:
        pl.semaphore_signal(barrier, inc=1, device_id={"grid": partner}, device_id_type=MESH)
    for near in (before, after):
        pl.semaphore_signal(barrier, inc=1, device_id={"dom": near}, device_id_type=MESH)
    pl.semaphore_wait(barrier, steps + 2)

    shift = pltpu.make_async_remote_copy(
        src_ref=v_ref.at[0], dst_ref=follow, send_sem=z_send, recv_sem=z_recv,
        device_id={"dom": before}, device_id_type=MESH,
    )
    shift.start()

    outer = tops[1]
    span = depth // outer
    outer_at = pick(projection_tables(outer), short[1])
    row_at = pick(row_tables(rows), short[0])
    weight = weight_ref[0].astype(jnp.float32)
    row_at = [[weight * entry for entry in line] for line in row_at]
    inner = inner_ref[short[2]] * inner_ref[SHORTFALLS + short[3]] * inner_ref[2 * SHORTFALLS + short[4]]
    lane = lane_ref[short[5]]

    def project(data):
        blocks = [split_dot(data[i * span : (i + 1) * span], left=inner) for i in range(outer)]
        mixed = []
        for i in range(outer):
            total = outer_at[i][0] * blocks[0]
            for j in range(1, outer):
                total = total + outer_at[i][j] * blocks[j]
            mixed.append(total)
        return split_dot(jnp.concatenate(mixed, axis=0), right=lane)

    def reduce_chunk(index, start, size):
        low, now = start, size
        lows = [low]
        taken = start
        for step in range(steps):
            half = now // 2
            keep = pl.multiple_of(low + bits[step] * half, 8)
            give = pl.multiple_of(low + (1 - bits[step]) * half, 8)
            copy = pltpu.make_async_remote_copy(
                src_ref=acc.at[pl.ds(give, half)], dst_ref=recv.at[pl.ds(taken, half)],
                send_sem=send_sem.at[index, step], recv_sem=recv_sem.at[index, step],
                device_id={"grid": partners[step]}, device_id_type=MESH,
            )
            copy.start()
            yield
            copy.wait()
            total = acc[pl.ds(keep, half), :] + recv[taken : taken + half, :]
            if step == steps - 1:
                out_ref[pl.ds(keep, half), :] = total
            else:
                acc[pl.ds(keep, half), :] = total
            taken += half
            low, now = keep, half
            lows.append(low)
        for step in range(steps - 1, -1, -1):
            mine = out_ref.at[pl.ds(lows[step + 1], now)]
            copy = pltpu.make_async_remote_copy(
                src_ref=mine, dst_ref=mine,
                send_sem=send_sem.at[index, 2 * steps - 1 - step],
                recv_sem=recv_sem.at[index, 2 * steps - 1 - step],
                device_id={"grid": partners[step]}, device_id_type=MESH,
            )
            copy.start()
            yield
            copy.wait()
            now *= 2

    first = project(v_ref[0])
    part[0] = first
    acc[0:depth, :] = row_at[0][0] * first
    head = reduce_chunk(0, 0, depth)
    next(head)
    for row in range(1, rows):
        part[row] = project(v_ref[row])
    next(head)
    shift.wait()
    part[rows] = project(follow[...])
    active = [head]
    for row in range(1, rows):
        total = row_at[row][0] * part[0]
        for source in range(1, rows + 1):
            total = total + row_at[row][source] * part[source]
        acc[row * depth : (row + 1) * depth, :] = total
        chunk = reduce_chunk(row, row * depth, depth)
        next(chunk)
        active.append(chunk)
    while active:
        active = [chunk for chunk in active if next(chunk, "end") != "end"]


def body(values, levels, coefficients):
    grid_data = values[0]
    level_row = levels[0]
    local_rows = grid_data.shape[0]
    extents = tuple(grid_data.shape[1:])
    groups, members = lax.axis_size("grid"), lax.axis_size("dom")
    lanes = extents[-1]
    depth = int(np.prod(extents[:-1]))

    tops = [local_rows * members] + list(extents)
    ones = [np.ones((points, points)) for points in extents[1:4]]
    inner = []
    for at, points in enumerate(extents[1:4]):
        for table in projection_tables(points):
            factors = ones[:at] + [table] + ones[at + 1 :]
            inner.append(np.kron(np.kron(factors[0], factors[1]), factors[2]))
    inner = jnp.asarray(np.stack(inner), jnp.bfloat16)
    lane = jnp.asarray(np.stack(projection_tables(lanes)).transpose(0, 2, 1), jnp.bfloat16)

    steps = groups.bit_length() - 1
    vmem = pl.BlockSpec(memory_space=pltpu.VMEM)
    smem = pl.BlockSpec(memory_space=pltpu.SMEM)
    combined = pl.pallas_call(
        functools.partial(kernel, groups, members, tops),
        out_shape=jax.ShapeDtypeStruct((local_rows * depth, lanes), jnp.float32),
        in_specs=[vmem, smem, smem, vmem, vmem],
        out_specs=vmem,
        scratch_shapes=[
            pltpu.VMEM((depth, lanes), jnp.float32),
            pltpu.VMEM((local_rows + 1, depth, lanes), jnp.float32),
            pltpu.VMEM((local_rows * depth, lanes), jnp.float32),
            pltpu.VMEM((local_rows * depth, lanes), jnp.float32),
            pltpu.SemaphoreType.DMA((local_rows, 2 * steps)),
            pltpu.SemaphoreType.DMA((local_rows, 2 * steps)),
            pltpu.SemaphoreType.DMA,
            pltpu.SemaphoreType.DMA,
        ],
        compiler_params=pltpu.CompilerParams(
            collective_id=0, has_side_effects=True, vmem_limit_bytes=40 * 1024 * 1024
        ),
    )(grid_data.reshape(local_rows, depth, lanes), levels, coefficients, inner, lane)
    holding = (
        split_rows_mask(level_row[0], local_rows, grid_data.ndim)
        * holding_mask(level_row[1:], extents)[None]
    )
    return (holding * combined.reshape(grid_data.shape))[None]


def solution(mesh):
    in_specs = (P("grid", "dom", None, None, None, None, None), P("grid", None), P("grid"))
    out_specs = P("grid", "dom", None, None, None, None, None)
    return jax.shard_map(body, mesh=mesh, in_specs=in_specs, out_specs=out_specs, check_vma=False)
```

```python
import functools

import jax
import jax.numpy as jnp
import numpy as np
from jax import lax
from jax.experimental import pallas as pl
from jax.experimental.pallas import tpu as pltpu
from jax.sharding import PartitionSpec as P

MESH = pl.DeviceIdType.MESH


def coarse_position(numerator, level_now):
    while numerator > 0 and numerator % 2 == 0:
        numerator = numerator // 2
        level_now = level_now - 1
    if numerator == 0:
        return 0
    return (1 << level_now - 1) + (numerator - 1) // 2


def parent_positions(position):
    level_now = position.bit_length()
    span_size = 1 << level_now - 1
    offset = position - span_size
    return [
        coarse_position(offset % span_size, level_now - 1),
        coarse_position((offset + 1) % span_size, level_now - 1),
    ]


def hier_table(points):
    matrix = np.eye(points)
    for position in range(1, points):
        for parent in parent_positions(position):
            matrix[position, parent] -= 0.5
    return matrix


def dehier_table(points):
    matrix = np.zeros((points, points))
    matrix[0, 0] = 1.0
    for position in range(1, points):
        row_now = np.zeros(points)
        row_now[position] = 1.0
        for parent in parent_positions(position):
            row_now = row_now + 0.5 * matrix[parent]
        matrix[position] = row_now
    return matrix


def local_hier(points):
    matrix = np.zeros((points, points + 1))
    matrix[0, 0] = 1.0
    for point in range(1, points):
        stride = point & -point
        matrix[point, point] = 1.0
        matrix[point, point - stride] -= 0.5
        matrix[point, point + stride] -= 0.5
    return matrix


def local_dehier(points):
    matrix = np.zeros((points + 1, points + 1))
    matrix[0, 0] = 1.0
    matrix[points, points] = 1.0
    stride = points // 2
    while stride >= 1:
        for point in range(stride, points, 2 * stride):
            row_now = np.zeros(points + 1)
            row_now[point] = 1.0
            matrix[point] = row_now + 0.5 * (matrix[point - stride] + matrix[point + stride])
        stride = stride // 2
    return matrix[:points]


SHORTFALLS = 3


def projection_tables(points):
    top = points.bit_length() - 1
    hier, dehier = hier_table(points), dehier_table(points)
    return [
        dehier @ np.diag((np.arange(points) < (1 << max(top - s, 0))).astype(np.float64)) @ hier
        for s in range(SHORTFALLS)
    ]


def row_tables(points):
    last = np.zeros((1, points + 1))
    last[0, points] = 1.0
    hier = np.concatenate([local_hier(points), last])
    result = []
    for s in range(SHORTFALLS):
        held = (np.arange(points + 1) % (1 << s) == 0).astype(np.float64)
        held[points] = 1.0
        result.append(local_dehier(points) @ np.diag(held) @ hier)
    return np.stack(result)


def split_dot(data, right=None, left=None):
    high = data.astype(jnp.bfloat16)
    low = (data - high.astype(jnp.float32)).astype(jnp.bfloat16)
    if right is not None:
        return jnp.dot(high, right, preferred_element_type=jnp.float32) + jnp.dot(
            low, right, preferred_element_type=jnp.float32
        )
    return jnp.dot(left, high, preferred_element_type=jnp.float32) + jnp.dot(
        left, low, preferred_element_type=jnp.float32
    )


def pick(tables, short):
    return [
        [jnp.where(short == 0, float(tables[0][i][j]),
                   jnp.where(short == 1, float(tables[1][i][j]), float(tables[2][i][j])))
         for j in range(len(tables[0][0]))]
        for i in range(len(tables[0]))
    ]


def kernel(groups, members, tops, v_ref, level_ref, weight_ref, inner_ref, lane_ref, out_ref,
           follow, part, acc, recv, gathered, send_sem, recv_sem, z_send, z_recv):
    rows, depth, lanes = v_ref.shape
    steps = groups.bit_length() - 1
    me = lax.axis_index("grid")
    dom = lax.axis_index("dom")
    core = lax.rem(me, 2)
    before = lax.rem(dom + members - 1, members)
    after = lax.rem(dom + 1, members)

    bits, partners = [], []
    for step in range(steps):
        up = 1 << step
        down = 1 << (steps - step) if step else 1
        bit_up = lax.rem(me // up, 2)
        bit_down = lax.rem(me // down, 2)
        bit = bit_up + core * (bit_down - bit_up)
        stride = up + core * (down - up)
        bits.append(bit)
        partners.append(me + (1 - 2 * bit) * stride)

    short = [
        jnp.clip(top.bit_length() - 1 - level_ref[0, k], 0, SHORTFALLS - 1) for k, top in enumerate(tops)
    ]

    barrier = pltpu.get_barrier_semaphore()
    for partner in partners:
        pl.semaphore_signal(barrier, inc=1, device_id={"grid": partner}, device_id_type=MESH)
    for near in (before, after):
        pl.semaphore_signal(barrier, inc=1, device_id={"dom": near}, device_id_type=MESH)
    pl.semaphore_wait(barrier, steps + 2)

    shift = pltpu.make_async_remote_copy(
        src_ref=v_ref.at[0], dst_ref=follow, send_sem=z_send, recv_sem=z_recv,
        device_id={"dom": before}, device_id_type=MESH,
    )
    shift.start()

    outer = tops[1]
    span = depth // outer
    outer_at = pick(projection_tables(outer), short[1])
    row_at = pick(row_tables(rows), short[0])
    weight = weight_ref[0].astype(jnp.float32)
    row_at = [[weight * entry for entry in line] for line in row_at]
    inner = inner_ref[short[2]] * inner_ref[SHORTFALLS + short[3]] * inner_ref[2 * SHORTFALLS + short[4]]
    lane = lane_ref[short[5]]

    def project(data):
        blocks = [split_dot(data[i * span : (i + 1) * span], left=inner) for i in range(outer)]
        mixed = []
        for i in range(outer):
            total = outer_at[i][0] * blocks[0]
            for j in range(1, outer):
                total = total + outer_at[i][j] * blocks[j]
            mixed.append(total)
        return split_dot(jnp.concatenate(mixed, axis=0), right=lane)

    def reduce_chunk(index, start, size):
        low, now = start, size
        lows = [low]
        taken = start
        for step in range(steps):
            half = now // 2
            keep = pl.multiple_of(low + bits[step] * half, 8)
            give = pl.multiple_of(low + (1 - bits[step]) * half, 8)
            copy = pltpu.make_async_remote_copy(
                src_ref=acc.at[pl.ds(give, half)], dst_ref=recv.at[pl.ds(taken, half)],
                send_sem=send_sem.at[index, step], recv_sem=recv_sem.at[index, step],
                device_id={"grid": partners[step]}, device_id_type=MESH,
            )
            copy.start()
            yield
            copy.wait()
            total = acc[pl.ds(keep, half), :] + recv[taken : taken + half, :]
            if step == steps - 1:
                gathered[pl.ds(keep, half), :] = total
            else:
                acc[pl.ds(keep, half), :] = total
            taken += half
            low, now = keep, half
            lows.append(low)
        for step in range(steps - 1, -1, -1):
            mine = gathered.at[pl.ds(lows[step + 1], now)]
            copy = pltpu.make_async_remote_copy(
                src_ref=mine, dst_ref=mine,
                send_sem=send_sem.at[index, 2 * steps - 1 - step],
                recv_sem=recv_sem.at[index, 2 * steps - 1 - step],
                device_id={"grid": partners[step]}, device_id_type=MESH,
            )
            copy.start()
            yield
            copy.wait()
            now *= 2

    place = lax.broadcasted_iota(jnp.int32, (depth, lanes), 0)
    inside = lax.broadcasted_iota(jnp.int32, (depth, lanes), 1) < (lanes >> short[5])
    below = depth
    for k in range(1, 5):
        below //= tops[k]
        inside &= ((place // below) % tops[k]) < (tops[k] >> short[k])
    held = inside.astype(jnp.float32)

    first = project(v_ref[0])
    part[0] = first
    acc[0:depth, :] = row_at[0][0] * first
    head = reduce_chunk(0, 0, depth)
    next(head)
    for row in range(1, rows):
        part[row] = project(v_ref[row])
    next(head)
    shift.wait()
    part[rows] = project(follow[...])
    active = [head]
    for row in range(1, rows):
        total = row_at[row][0] * part[0]
        for source in range(1, rows + 1):
            total = total + row_at[row][source] * part[source]
        acc[row * depth : (row + 1) * depth, :] = total
        chunk = reduce_chunk(row, row * depth, depth)
        next(chunk)
        active.append(chunk)
    while active:
        active = [chunk for chunk in active if next(chunk, "end") != "end"]
    for row in range(rows):
        here = jnp.where((row & ((1 << short[0]) - 1)) == 0, 1.0, 0.0)
        out_ref[row * depth : (row + 1) * depth, :] = here * held * gathered[row * depth : (row + 1) * depth, :]


def body(values, levels, coefficients):
    grid_data = values[0]
    level_row = levels[0]
    local_rows = grid_data.shape[0]
    extents = tuple(grid_data.shape[1:])
    groups, members = lax.axis_size("grid"), lax.axis_size("dom")
    lanes = extents[-1]
    depth = int(np.prod(extents[:-1]))

    tops = [local_rows * members] + list(extents)
    ones = [np.ones((points, points)) for points in extents[1:4]]
    inner = []
    for at, points in enumerate(extents[1:4]):
        for table in projection_tables(points):
            factors = ones[:at] + [table] + ones[at + 1 :]
            inner.append(np.kron(np.kron(factors[0], factors[1]), factors[2]))
    inner = jnp.asarray(np.stack(inner), jnp.bfloat16)
    lane = jnp.asarray(np.stack(projection_tables(lanes)).transpose(0, 2, 1), jnp.bfloat16)

    steps = groups.bit_length() - 1
    vmem = pl.BlockSpec(memory_space=pltpu.VMEM)
    smem = pl.BlockSpec(memory_space=pltpu.SMEM)
    combined = pl.pallas_call(
        functools.partial(kernel, groups, members, tops),
        out_shape=jax.ShapeDtypeStruct((local_rows * depth, lanes), jnp.float32),
        in_specs=[vmem, smem, smem, vmem, vmem],
        out_specs=vmem,
        scratch_shapes=[
            pltpu.VMEM((depth, lanes), jnp.float32),
            pltpu.VMEM((local_rows + 1, depth, lanes), jnp.float32),
            pltpu.VMEM((local_rows * depth, lanes), jnp.float32),
            pltpu.VMEM((local_rows * depth, lanes), jnp.float32),
            pltpu.VMEM((local_rows * depth, lanes), jnp.float32),
            pltpu.SemaphoreType.DMA((local_rows, 2 * steps)),
            pltpu.SemaphoreType.DMA((local_rows, 2 * steps)),
            pltpu.SemaphoreType.DMA,
            pltpu.SemaphoreType.DMA,
        ],
        compiler_params=pltpu.CompilerParams(
            collective_id=0, has_side_effects=True, vmem_limit_bytes=40 * 1024 * 1024
        ),
    )(grid_data.reshape(local_rows, depth, lanes), levels, coefficients, inner, lane)
    return combined.reshape(grid_data.shape)[None]


def solution(mesh):
    in_specs = (P("grid", "dom", None, None, None, None, None), P("grid", None), P("grid"))
    out_specs = P("grid", "dom", None, None, None, None, None)
    return jax.shard_map(body, mesh=mesh, in_specs=in_specs, out_specs=out_specs, check_vma=False)
```

```python
import functools

import jax
import jax.numpy as jnp
import numpy as np
from jax import lax
from jax.experimental import pallas as pl
from jax.experimental.pallas import tpu as pltpu
from jax.sharding import PartitionSpec as P

MESH = pl.DeviceIdType.MESH


def coarse_position(numerator, level_now):
    while numerator > 0 and numerator % 2 == 0:
        numerator = numerator // 2
        level_now = level_now - 1
    if numerator == 0:
        return 0
    return (1 << level_now - 1) + (numerator - 1) // 2


def parent_positions(position):
    level_now = position.bit_length()
    span_size = 1 << level_now - 1
    offset = position - span_size
    return [
        coarse_position(offset % span_size, level_now - 1),
        coarse_position((offset + 1) % span_size, level_now - 1),
    ]


def hier_table(points):
    matrix = np.eye(points)
    for position in range(1, points):
        for parent in parent_positions(position):
            matrix[position, parent] -= 0.5
    return matrix


def dehier_table(points):
    matrix = np.zeros((points, points))
    matrix[0, 0] = 1.0
    for position in range(1, points):
        row_now = np.zeros(points)
        row_now[position] = 1.0
        for parent in parent_positions(position):
            row_now = row_now + 0.5 * matrix[parent]
        matrix[position] = row_now
    return matrix


def local_hier(points):
    matrix = np.zeros((points, points + 1))
    matrix[0, 0] = 1.0
    for point in range(1, points):
        stride = point & -point
        matrix[point, point] = 1.0
        matrix[point, point - stride] -= 0.5
        matrix[point, point + stride] -= 0.5
    return matrix


def local_dehier(points):
    matrix = np.zeros((points + 1, points + 1))
    matrix[0, 0] = 1.0
    matrix[points, points] = 1.0
    stride = points // 2
    while stride >= 1:
        for point in range(stride, points, 2 * stride):
            row_now = np.zeros(points + 1)
            row_now[point] = 1.0
            matrix[point] = row_now + 0.5 * (matrix[point - stride] + matrix[point + stride])
        stride = stride // 2
    return matrix[:points]


SHORTFALLS = 3


def projection_tables(points):
    top = points.bit_length() - 1
    hier, dehier = hier_table(points), dehier_table(points)
    return [
        dehier @ np.diag((np.arange(points) < (1 << max(top - s, 0))).astype(np.float64)) @ hier
        for s in range(SHORTFALLS)
    ]


def row_tables(points):
    last = np.zeros((1, points + 1))
    last[0, points] = 1.0
    hier = np.concatenate([local_hier(points), last])
    result = []
    for s in range(SHORTFALLS):
        held = (np.arange(points + 1) % (1 << s) == 0).astype(np.float64)
        held[points] = 1.0
        result.append(local_dehier(points) @ np.diag(held) @ hier)
    return np.stack(result)


def split_dot(data, right=None, left=None):
    high = data.astype(jnp.bfloat16)
    low = (data - high.astype(jnp.float32)).astype(jnp.bfloat16)
    if right is not None:
        return jnp.dot(high, right, preferred_element_type=jnp.float32) + jnp.dot(
            low, right, preferred_element_type=jnp.float32
        )
    return jnp.dot(left, high, preferred_element_type=jnp.float32) + jnp.dot(
        left, low, preferred_element_type=jnp.float32
    )


def pick(tables, short):
    return [
        [jnp.where(short == 0, float(tables[0][i][j]),
                   jnp.where(short == 1, float(tables[1][i][j]), float(tables[2][i][j])))
         for j in range(len(tables[0][0]))]
        for i in range(len(tables[0]))
    ]


def kernel(groups, members, tops, v_ref, level_ref, weight_ref, inner_ref, lane_ref, out_ref,
           follow, part, acc, recv, gathered, send_sem, recv_sem, z_send, z_recv):
    rows, depth, lanes = v_ref.shape
    steps = groups.bit_length() - 1
    me = lax.axis_index("grid")
    dom = lax.axis_index("dom")
    core = lax.rem(me, 2)
    before = lax.rem(dom + members - 1, members)
    after = lax.rem(dom + 1, members)

    bits, partners = [], []
    for step in range(steps):
        up = 1 << step
        down = 1 << (steps - step) if step else 1
        bit_up = lax.rem(me // up, 2)
        bit_down = lax.rem(me // down, 2)
        bit = bit_up + core * (bit_down - bit_up)
        stride = up + core * (down - up)
        bits.append(bit)
        partners.append(me + (1 - 2 * bit) * stride)

    short = [
        jnp.clip(top.bit_length() - 1 - level_ref[0, k], 0, SHORTFALLS - 1) for k, top in enumerate(tops)
    ]

    barrier = pltpu.get_barrier_semaphore()
    for partner in partners:
        pl.semaphore_signal(barrier, inc=1, device_id={"grid": partner}, device_id_type=MESH)
    for near in (before, after):
        pl.semaphore_signal(barrier, inc=1, device_id={"dom": near}, device_id_type=MESH)
    pl.semaphore_wait(barrier, steps + 2)

    outer = tops[1]
    span = depth // outer
    shifts = []
    for i in range(outer):
        piece = pl.ds(i * span, span)
        shift = pltpu.make_async_remote_copy(
            src_ref=v_ref.at[0, piece], dst_ref=follow.at[piece],
            send_sem=z_send.at[i], recv_sem=z_recv.at[i],
            device_id={"dom": before}, device_id_type=MESH,
        )
        shift.start()
        shifts.append(shift)
    outer_at = pick(projection_tables(outer), short[1])
    row_at = pick(row_tables(rows), short[0])
    weight = weight_ref[0].astype(jnp.float32)
    row_at = [[weight * entry for entry in line] for line in row_at]
    inner = inner_ref[short[2]] * inner_ref[SHORTFALLS + short[3]] * inner_ref[2 * SHORTFALLS + short[4]]
    lane = lane_ref[short[5]]

    def project(data):
        blocks = [split_dot(data[i * span : (i + 1) * span], left=inner) for i in range(outer)]
        mixed = []
        for i in range(outer):
            total = outer_at[i][0] * blocks[0]
            for j in range(1, i + 1):
                total = total + outer_at[i][j] * blocks[j]
            mixed.append(total)
        return split_dot(jnp.concatenate(mixed, axis=0), right=lane)

    def finish(index):
        if index == 0:
            out_ref[0:depth, :] = held * gathered[0:depth, :]
            return
        block = index - 1
        for row in range(1, rows):
            at = depth + (block * (rows - 1) + row - 1) * span
            here = jnp.where((row & ((1 << short[0]) - 1)) == 0, 1.0, 0.0)
            out_ref[row * depth + block * span : row * depth + (block + 1) * span, :] = (
                here * held[block * span : (block + 1) * span] * gathered[at : at + span, :]
            )

    def reduce_chunk(index, start, size):
        low, now = start, size
        lows = [low]
        taken = start
        for step in range(steps):
            half = now // 2
            keep = pl.multiple_of(low + bits[step] * half, 8)
            give = pl.multiple_of(low + (1 - bits[step]) * half, 8)
            copy = pltpu.make_async_remote_copy(
                src_ref=acc.at[pl.ds(give, half)], dst_ref=recv.at[pl.ds(taken, half)],
                send_sem=send_sem.at[index, step], recv_sem=recv_sem.at[index, step],
                device_id={"grid": partners[step]}, device_id_type=MESH,
            )
            copy.start()
            yield
            copy.wait()
            total = acc[pl.ds(keep, half), :] + recv[taken : taken + half, :]
            if step == steps - 1:
                gathered[pl.ds(keep, half), :] = total
            else:
                acc[pl.ds(keep, half), :] = total
            taken += half
            low, now = keep, half
            lows.append(low)
        for step in range(steps - 1, -1, -1):
            mine = gathered.at[pl.ds(lows[step + 1], now)]
            copy = pltpu.make_async_remote_copy(
                src_ref=mine, dst_ref=mine,
                send_sem=send_sem.at[index, 2 * steps - 1 - step],
                recv_sem=recv_sem.at[index, 2 * steps - 1 - step],
                device_id={"grid": partners[step]}, device_id_type=MESH,
            )
            copy.start()
            yield
            copy.wait()
            now *= 2
        finish(index)

    place = lax.broadcasted_iota(jnp.int32, (depth, lanes), 0)
    inside = lax.broadcasted_iota(jnp.int32, (depth, lanes), 1) < (lanes >> short[5])
    below = depth
    for k in range(1, 5):
        below //= tops[k]
        inside &= ((place // below) % tops[k]) < (tops[k] >> short[k])
    held = inside.astype(jnp.float32)

    first = project(v_ref[0])
    part[0] = first
    acc[0:depth, :] = row_at[0][0] * first
    head = reduce_chunk(0, 0, depth)
    next(head)
    for row in range(1, rows):
        part[row] = project(v_ref[row])
    active = [head]
    taken = []
    for block in range(outer):
        shifts[block].wait()
        here = slice(block * span, (block + 1) * span)
        taken.append(split_dot(follow[here, :], left=inner))
        total = outer_at[block][0] * taken[0]
        for j in range(1, block + 1):
            total = total + outer_at[block][j] * taken[j]
        ahead = split_dot(total, right=lane)
        for row in range(1, rows):
            total = row_at[row][rows] * ahead
            for source in range(rows):
                total = total + row_at[row][source] * part[source, here, :]
            at = depth + (block * (rows - 1) + row - 1) * span
            acc[at : at + span, :] = total
        width = (rows - 1) * span
        chunk = reduce_chunk(block + 1, depth + block * width, width)
        next(chunk)
        active = [each for each in active if next(each, "end") != "end"]
        active.append(chunk)
    while active:
        active = [chunk for chunk in active if next(chunk, "end") != "end"]


def body(values, levels, coefficients):
    grid_data = values[0]
    level_row = levels[0]
    local_rows = grid_data.shape[0]
    extents = tuple(grid_data.shape[1:])
    groups, members = lax.axis_size("grid"), lax.axis_size("dom")
    lanes = extents[-1]
    depth = int(np.prod(extents[:-1]))

    tops = [local_rows * members] + list(extents)
    ones = [np.ones((points, points)) for points in extents[1:4]]
    inner = []
    for at, points in enumerate(extents[1:4]):
        for table in projection_tables(points):
            factors = ones[:at] + [table] + ones[at + 1 :]
            inner.append(np.kron(np.kron(factors[0], factors[1]), factors[2]))
    inner = jnp.asarray(np.stack(inner), jnp.bfloat16)
    lane = jnp.asarray(np.stack(projection_tables(lanes)).transpose(0, 2, 1), jnp.bfloat16)

    steps = groups.bit_length() - 1
    vmem = pl.BlockSpec(memory_space=pltpu.VMEM)
    smem = pl.BlockSpec(memory_space=pltpu.SMEM)
    combined = pl.pallas_call(
        functools.partial(kernel, groups, members, tops),
        out_shape=jax.ShapeDtypeStruct((local_rows * depth, lanes), jnp.float32),
        in_specs=[vmem, smem, smem, vmem, vmem],
        out_specs=vmem,
        scratch_shapes=[
            pltpu.VMEM((depth, lanes), jnp.float32),
            pltpu.VMEM((local_rows, depth, lanes), jnp.float32),
            pltpu.VMEM((local_rows * depth, lanes), jnp.float32),
            pltpu.VMEM((local_rows * depth, lanes), jnp.float32),
            pltpu.VMEM((local_rows * depth, lanes), jnp.float32),
            pltpu.SemaphoreType.DMA((extents[0] + 1, 2 * steps)),
            pltpu.SemaphoreType.DMA((extents[0] + 1, 2 * steps)),
            pltpu.SemaphoreType.DMA((extents[0],)),
            pltpu.SemaphoreType.DMA((extents[0],)),
        ],
        compiler_params=pltpu.CompilerParams(
            collective_id=0, has_side_effects=True, vmem_limit_bytes=40 * 1024 * 1024
        ),
    )(grid_data.reshape(local_rows, depth, lanes), levels, coefficients, inner, lane)
    return combined.reshape(grid_data.shape)[None]


def solution(mesh):
    in_specs = (P("grid", "dom", None, None, None, None, None), P("grid", None), P("grid"))
    out_specs = P("grid", "dom", None, None, None, None, None)
    return jax.shard_map(body, mesh=mesh, in_specs=in_specs, out_specs=out_specs, check_vma=False)
```

```python
import functools

import jax
import jax.numpy as jnp
import numpy as np
from jax import lax
from jax.experimental import pallas as pl
from jax.experimental.pallas import tpu as pltpu
from jax.sharding import PartitionSpec as P

MESH = pl.DeviceIdType.MESH


def coarse_position(numerator, level_now):
    while numerator > 0 and numerator % 2 == 0:
        numerator = numerator // 2
        level_now = level_now - 1
    if numerator == 0:
        return 0
    return (1 << level_now - 1) + (numerator - 1) // 2


def parent_positions(position):
    level_now = position.bit_length()
    span_size = 1 << level_now - 1
    offset = position - span_size
    return [
        coarse_position(offset % span_size, level_now - 1),
        coarse_position((offset + 1) % span_size, level_now - 1),
    ]


def hier_table(points):
    matrix = np.eye(points)
    for position in range(1, points):
        for parent in parent_positions(position):
            matrix[position, parent] -= 0.5
    return matrix


def dehier_table(points):
    matrix = np.zeros((points, points))
    matrix[0, 0] = 1.0
    for position in range(1, points):
        row_now = np.zeros(points)
        row_now[position] = 1.0
        for parent in parent_positions(position):
            row_now = row_now + 0.5 * matrix[parent]
        matrix[position] = row_now
    return matrix


def local_hier(points):
    matrix = np.zeros((points, points + 1))
    matrix[0, 0] = 1.0
    for point in range(1, points):
        stride = point & -point
        matrix[point, point] = 1.0
        matrix[point, point - stride] -= 0.5
        matrix[point, point + stride] -= 0.5
    return matrix


def local_dehier(points):
    matrix = np.zeros((points + 1, points + 1))
    matrix[0, 0] = 1.0
    matrix[points, points] = 1.0
    stride = points // 2
    while stride >= 1:
        for point in range(stride, points, 2 * stride):
            row_now = np.zeros(points + 1)
            row_now[point] = 1.0
            matrix[point] = row_now + 0.5 * (matrix[point - stride] + matrix[point + stride])
        stride = stride // 2
    return matrix[:points]


SHORTFALLS = 3


def projection_tables(points):
    top = points.bit_length() - 1
    hier, dehier = hier_table(points), dehier_table(points)
    return [
        dehier @ np.diag((np.arange(points) < (1 << max(top - s, 0))).astype(np.float64)) @ hier
        for s in range(SHORTFALLS)
    ]


def row_tables(points):
    last = np.zeros((1, points + 1))
    last[0, points] = 1.0
    hier = np.concatenate([local_hier(points), last])
    result = []
    for s in range(SHORTFALLS):
        held = (np.arange(points + 1) % (1 << s) == 0).astype(np.float64)
        held[points] = 1.0
        result.append(local_dehier(points) @ np.diag(held) @ hier)
    return np.stack(result)


def split_dot(data, right=None, left=None):
    high = data.astype(jnp.bfloat16)
    low = (data - high.astype(jnp.float32)).astype(jnp.bfloat16)
    if right is not None:
        return jnp.dot(high, right, preferred_element_type=jnp.float32) + jnp.dot(
            low, right, preferred_element_type=jnp.float32
        )
    return jnp.dot(left, high, preferred_element_type=jnp.float32) + jnp.dot(
        left, low, preferred_element_type=jnp.float32
    )


def pick(tables, short):
    return [
        [jnp.where(short == 0, float(tables[0][i][j]),
                   jnp.where(short == 1, float(tables[1][i][j]), float(tables[2][i][j])))
         for j in range(len(tables[0][0]))]
        for i in range(len(tables[0]))
    ]


def kernel(groups, members, tops, v_hbm, level_ref, weight_ref, inner_hbm, lane_hbm, out_ref,
           v_ref, inner_ref, lane_ref, load_sem, follow, part, acc, recv, gathered, send_sem, recv_sem, z_send, z_recv):
    rows, depth, lanes = v_ref.shape
    loads = [
        pltpu.make_async_copy(v_hbm.at[0], v_ref.at[0], load_sem.at[0]),
        pltpu.make_async_copy(inner_hbm, inner_ref, load_sem.at[rows]),
        pltpu.make_async_copy(lane_hbm, lane_ref, load_sem.at[rows + 1]),
    ]
    later = [pltpu.make_async_copy(v_hbm.at[row], v_ref.at[row], load_sem.at[row]) for row in range(1, rows)]
    for load in loads + later:
        load.start()
    steps = groups.bit_length() - 1
    me = lax.axis_index("grid")
    dom = lax.axis_index("dom")
    core = lax.rem(me, 2)
    before = lax.rem(dom + members - 1, members)
    after = lax.rem(dom + 1, members)

    bits, partners = [], []
    for step in range(steps):
        up = 1 << step
        down = 1 << (steps - step) if step else 1
        bit_up = lax.rem(me // up, 2)
        bit_down = lax.rem(me // down, 2)
        bit = bit_up + core * (bit_down - bit_up)
        stride = up + core * (down - up)
        bits.append(bit)
        partners.append(me + (1 - 2 * bit) * stride)

    short = [
        jnp.clip(top.bit_length() - 1 - level_ref[0, k], 0, SHORTFALLS - 1) for k, top in enumerate(tops)
    ]

    barrier = pltpu.get_barrier_semaphore()
    for partner in partners:
        pl.semaphore_signal(barrier, inc=1, device_id={"grid": partner}, device_id_type=MESH)
    for near in (before, after):
        pl.semaphore_signal(barrier, inc=1, device_id={"dom": near}, device_id_type=MESH)
    pl.semaphore_wait(barrier, steps + 2)

    shift = pltpu.make_async_remote_copy(
        src_ref=v_hbm.at[0], dst_ref=follow, send_sem=z_send, recv_sem=z_recv,
        device_id={"dom": before}, device_id_type=MESH,
    )
    shift.start()

    outer = tops[1]
    span = depth // outer
    outer_at = pick(projection_tables(outer), short[1])
    row_at = pick(row_tables(rows), short[0])
    weight = weight_ref[0].astype(jnp.float32)
    row_at = [[weight * entry for entry in line] for line in row_at]
    for load in loads:
        load.wait()
    inner = inner_ref[short[2]] * inner_ref[SHORTFALLS + short[3]] * inner_ref[2 * SHORTFALLS + short[4]]
    lane = lane_ref[short[5]]

    def project(data):
        blocks = [split_dot(data[i * span : (i + 1) * span], left=inner) for i in range(outer)]
        mixed = []
        for i in range(outer):
            total = outer_at[i][0] * blocks[0]
            for j in range(1, outer):
                total = total + outer_at[i][j] * blocks[j]
            mixed.append(total)
        return split_dot(jnp.concatenate(mixed, axis=0), right=lane)

    def reduce_chunk(index, start, size):
        low, now = start, size
        lows = [low]
        taken = start
        for step in range(steps):
            half = now // 2
            keep = pl.multiple_of(low + bits[step] * half, 8)
            give = pl.multiple_of(low + (1 - bits[step]) * half, 8)
            copy = pltpu.make_async_remote_copy(
                src_ref=acc.at[pl.ds(give, half)], dst_ref=recv.at[pl.ds(taken, half)],
                send_sem=send_sem.at[index, step], recv_sem=recv_sem.at[index, step],
                device_id={"grid": partners[step]}, device_id_type=MESH,
            )
            copy.start()
            yield
            copy.wait()
            total = acc[pl.ds(keep, half), :] + recv[taken : taken + half, :]
            if step == steps - 1:
                gathered[pl.ds(keep, half), :] = total
            else:
                acc[pl.ds(keep, half), :] = total
            taken += half
            low, now = keep, half
            lows.append(low)
        for step in range(steps - 1, -1, -1):
            mine = gathered.at[pl.ds(lows[step + 1], now)]
            copy = pltpu.make_async_remote_copy(
                src_ref=mine, dst_ref=mine,
                send_sem=send_sem.at[index, 2 * steps - 1 - step],
                recv_sem=recv_sem.at[index, 2 * steps - 1 - step],
                device_id={"grid": partners[step]}, device_id_type=MESH,
            )
            copy.start()
            yield
            copy.wait()
            now *= 2

    place = lax.broadcasted_iota(jnp.int32, (depth, lanes), 0)
    inside = lax.broadcasted_iota(jnp.int32, (depth, lanes), 1) < (lanes >> short[5])
    below = depth
    for k in range(1, 5):
        below //= tops[k]
        inside &= ((place // below) % tops[k]) < (tops[k] >> short[k])
    held = inside.astype(jnp.float32)

    first = project(v_ref[0])
    part[0] = first
    acc[0:depth, :] = row_at[0][0] * first
    head = reduce_chunk(0, 0, depth)
    next(head)
    for row in range(1, rows):
        later[row - 1].wait()
        part[row] = project(v_ref[row])
        next(head)
    next(head)
    shift.wait()
    part[rows] = project(follow[...])
    active = [head]
    for row in range(1, rows):
        total = row_at[row][0] * part[0]
        for source in range(1, rows + 1):
            total = total + row_at[row][source] * part[source]
        acc[row * depth : (row + 1) * depth, :] = total
        chunk = reduce_chunk(row, row * depth, depth)
        next(chunk)
        active.append(chunk)
    while active:
        active = [chunk for chunk in active if next(chunk, "end") != "end"]
    for row in range(rows):
        here = jnp.where((row & ((1 << short[0]) - 1)) == 0, 1.0, 0.0)
        out_ref[row * depth : (row + 1) * depth, :] = here * held * gathered[row * depth : (row + 1) * depth, :]


def body(values, levels, coefficients):
    grid_data = values[0]
    level_row = levels[0]
    local_rows = grid_data.shape[0]
    extents = tuple(grid_data.shape[1:])
    groups, members = lax.axis_size("grid"), lax.axis_size("dom")
    lanes = extents[-1]
    depth = int(np.prod(extents[:-1]))

    tops = [local_rows * members] + list(extents)
    ones = [np.ones((points, points)) for points in extents[1:4]]
    inner = []
    for at, points in enumerate(extents[1:4]):
        for table in projection_tables(points):
            factors = ones[:at] + [table] + ones[at + 1 :]
            inner.append(np.kron(np.kron(factors[0], factors[1]), factors[2]))
    inner = jnp.asarray(np.stack(inner), jnp.bfloat16)
    lane = jnp.asarray(np.stack(projection_tables(lanes)).transpose(0, 2, 1), jnp.bfloat16)

    steps = groups.bit_length() - 1
    vmem = pl.BlockSpec(memory_space=pltpu.VMEM)
    hbm = pl.BlockSpec(memory_space=pltpu.HBM)
    smem = pl.BlockSpec(memory_space=pltpu.SMEM)
    combined = pl.pallas_call(
        functools.partial(kernel, groups, members, tops),
        out_shape=jax.ShapeDtypeStruct((local_rows * depth, lanes), jnp.float32),
        in_specs=[hbm, smem, smem, hbm, hbm],
        out_specs=vmem,
        scratch_shapes=[
            pltpu.VMEM((local_rows, depth, lanes), jnp.float32),
            pltpu.VMEM(inner.shape, jnp.bfloat16),
            pltpu.VMEM(lane.shape, jnp.bfloat16),
            pltpu.SemaphoreType.DMA((local_rows + 2,)),
            pltpu.VMEM((depth, lanes), jnp.float32),
            pltpu.VMEM((local_rows + 1, depth, lanes), jnp.float32),
            pltpu.VMEM((local_rows * depth, lanes), jnp.float32),
            pltpu.VMEM((local_rows * depth, lanes), jnp.float32),
            pltpu.VMEM((local_rows * depth, lanes), jnp.float32),
            pltpu.SemaphoreType.DMA((local_rows, 2 * steps)),
            pltpu.SemaphoreType.DMA((local_rows, 2 * steps)),
            pltpu.SemaphoreType.DMA,
            pltpu.SemaphoreType.DMA,
        ],
        compiler_params=pltpu.CompilerParams(
            collective_id=0, has_side_effects=True, vmem_limit_bytes=61 * 1024 * 1024
        ),
    )(grid_data.reshape(local_rows, depth, lanes), levels, coefficients, inner, lane)
    return combined.reshape(grid_data.shape)[None]


def solution(mesh):
    in_specs = (P("grid", "dom", None, None, None, None, None), P("grid", None), P("grid"))
    out_specs = P("grid", "dom", None, None, None, None, None)
    return jax.shard_map(body, mesh=mesh, in_specs=in_specs, out_specs=out_specs, check_vma=False)
```

```python
import functools

import jax
import jax.numpy as jnp
import numpy as np
from jax import lax
from jax.experimental import pallas as pl
from jax.experimental.pallas import tpu as pltpu
from jax.sharding import PartitionSpec as P

MESH = pl.DeviceIdType.MESH


def coarse_position(numerator, level_now):
    while numerator > 0 and numerator % 2 == 0:
        numerator = numerator // 2
        level_now = level_now - 1
    if numerator == 0:
        return 0
    return (1 << level_now - 1) + (numerator - 1) // 2


def parent_positions(position):
    level_now = position.bit_length()
    span_size = 1 << level_now - 1
    offset = position - span_size
    return [
        coarse_position(offset % span_size, level_now - 1),
        coarse_position((offset + 1) % span_size, level_now - 1),
    ]


def hier_table(points):
    matrix = np.eye(points)
    for position in range(1, points):
        for parent in parent_positions(position):
            matrix[position, parent] -= 0.5
    return matrix


def dehier_table(points):
    matrix = np.zeros((points, points))
    matrix[0, 0] = 1.0
    for position in range(1, points):
        row_now = np.zeros(points)
        row_now[position] = 1.0
        for parent in parent_positions(position):
            row_now = row_now + 0.5 * matrix[parent]
        matrix[position] = row_now
    return matrix


def local_hier(points):
    matrix = np.zeros((points, points + 1))
    matrix[0, 0] = 1.0
    for point in range(1, points):
        stride = point & -point
        matrix[point, point] = 1.0
        matrix[point, point - stride] -= 0.5
        matrix[point, point + stride] -= 0.5
    return matrix


def local_dehier(points):
    matrix = np.zeros((points + 1, points + 1))
    matrix[0, 0] = 1.0
    matrix[points, points] = 1.0
    stride = points // 2
    while stride >= 1:
        for point in range(stride, points, 2 * stride):
            row_now = np.zeros(points + 1)
            row_now[point] = 1.0
            matrix[point] = row_now + 0.5 * (matrix[point - stride] + matrix[point + stride])
        stride = stride // 2
    return matrix[:points]


SHORTFALLS = 3


def projection_tables(points):
    top = points.bit_length() - 1
    hier, dehier = hier_table(points), dehier_table(points)
    return [
        dehier @ np.diag((np.arange(points) < (1 << max(top - s, 0))).astype(np.float64)) @ hier
        for s in range(SHORTFALLS)
    ]


def row_tables(points):
    last = np.zeros((1, points + 1))
    last[0, points] = 1.0
    hier = np.concatenate([local_hier(points), last])
    result = []
    for s in range(SHORTFALLS):
        held = (np.arange(points + 1) % (1 << s) == 0).astype(np.float64)
        held[points] = 1.0
        result.append(local_dehier(points) @ np.diag(held) @ hier)
    return np.stack(result)


def split_dot(data, right=None, left=None):
    high = data.astype(jnp.bfloat16)
    low = (data - high.astype(jnp.float32)).astype(jnp.bfloat16)
    both = jnp.concatenate([high, low], axis=1)
    if right is not None:
        return jnp.dot(both, jnp.concatenate([right, right], axis=0), preferred_element_type=jnp.float32)
    result = jnp.dot(left, both, preferred_element_type=jnp.float32)
    return result[:, : data.shape[1]] + result[:, data.shape[1] :]


def pick(tables, short):
    return [
        [jnp.where(short == 0, float(tables[0][i][j]),
                   jnp.where(short == 1, float(tables[1][i][j]), float(tables[2][i][j])))
         for j in range(len(tables[0][0]))]
        for i in range(len(tables[0]))
    ]


def kernel(groups, members, tops, v_ref, level_ref, weight_ref, inner_ref, lane_ref, out_ref,
           follow, part, acc, recv, gathered, send_sem, recv_sem, z_send, z_recv):
    rows, depth, lanes = v_ref.shape
    steps = groups.bit_length() - 1
    me = lax.axis_index("grid")
    dom = lax.axis_index("dom")
    core = lax.rem(me, 2)
    before = lax.rem(dom + members - 1, members)
    after = lax.rem(dom + 1, members)

    bits, partners = [], []
    for step in range(steps):
        up = 1 << step
        down = 1 << (steps - step) if step else 1
        bit_up = lax.rem(me // up, 2)
        bit_down = lax.rem(me // down, 2)
        bit = bit_up + core * (bit_down - bit_up)
        stride = up + core * (down - up)
        bits.append(bit)
        partners.append(me + (1 - 2 * bit) * stride)

    short = [
        jnp.clip(top.bit_length() - 1 - level_ref[0, k], 0, SHORTFALLS - 1) for k, top in enumerate(tops)
    ]

    barrier = pltpu.get_barrier_semaphore()
    for partner in partners:
        pl.semaphore_signal(barrier, inc=1, device_id={"grid": partner}, device_id_type=MESH)
    for near in (before, after):
        pl.semaphore_signal(barrier, inc=1, device_id={"dom": near}, device_id_type=MESH)
    pl.semaphore_wait(barrier, steps + 2)

    shift = pltpu.make_async_remote_copy(
        src_ref=v_ref.at[0], dst_ref=follow, send_sem=z_send, recv_sem=z_recv,
        device_id={"dom": before}, device_id_type=MESH,
    )
    shift.start()

    outer = tops[1]
    span = depth // outer
    outer_at = pick(projection_tables(outer), short[1])
    row_at = pick(row_tables(rows), short[0])
    weight = weight_ref[0].astype(jnp.float32)
    row_at = [[weight * entry for entry in line] for line in row_at]
    inner = inner_ref[short[2]] * inner_ref[SHORTFALLS + short[3]] * inner_ref[2 * SHORTFALLS + short[4]]
    lane = lane_ref[short[5]]

    def project(data):
        blocks = [split_dot(data[i * span : (i + 1) * span], left=inner) for i in range(outer)]
        mixed = []
        for i in range(outer):
            total = outer_at[i][0] * blocks[0]
            for j in range(1, outer):
                total = total + outer_at[i][j] * blocks[j]
            mixed.append(total)
        return split_dot(jnp.concatenate(mixed, axis=0), right=lane)

    def reduce_chunk(index, start, size):
        low, now = start, size
        lows = [low]
        taken = start
        for step in range(steps):
            half = now // 2
            keep = pl.multiple_of(low + bits[step] * half, 8)
            give = pl.multiple_of(low + (1 - bits[step]) * half, 8)
            copy = pltpu.make_async_remote_copy(
                src_ref=acc.at[pl.ds(give, half)], dst_ref=recv.at[pl.ds(taken, half)],
                send_sem=send_sem.at[index, step], recv_sem=recv_sem.at[index, step],
                device_id={"grid": partners[step]}, device_id_type=MESH,
            )
            copy.start()
            yield
            copy.wait()
            total = acc[pl.ds(keep, half), :] + recv[taken : taken + half, :]
            if step == steps - 1:
                gathered[pl.ds(keep, half), :] = total
            else:
                acc[pl.ds(keep, half), :] = total
            taken += half
            low, now = keep, half
            lows.append(low)
        for step in range(steps - 1, -1, -1):
            mine = gathered.at[pl.ds(lows[step + 1], now)]
            copy = pltpu.make_async_remote_copy(
                src_ref=mine, dst_ref=mine,
                send_sem=send_sem.at[index, 2 * steps - 1 - step],
                recv_sem=recv_sem.at[index, 2 * steps - 1 - step],
                device_id={"grid": partners[step]}, device_id_type=MESH,
            )
            copy.start()
            yield
            copy.wait()
            now *= 2

    place = lax.broadcasted_iota(jnp.int32, (depth, lanes), 0)
    inside = lax.broadcasted_iota(jnp.int32, (depth, lanes), 1) < (lanes >> short[5])
    below = depth
    for k in range(1, 5):
        below //= tops[k]
        inside &= ((place // below) % tops[k]) < (tops[k] >> short[k])
    held = inside.astype(jnp.float32)

    first = project(v_ref[0])
    part[0] = first
    acc[0:depth, :] = row_at[0][0] * first
    head = reduce_chunk(0, 0, depth)
    next(head)
    for row in range(1, rows):
        part[row] = project(v_ref[row])
    next(head)
    shift.wait()
    part[rows] = project(follow[...])
    active = [head]
    for row in range(1, rows):
        total = row_at[row][0] * part[0]
        for source in range(1, rows + 1):
            total = total + row_at[row][source] * part[source]
        acc[row * depth : (row + 1) * depth, :] = total
        chunk = reduce_chunk(row, row * depth, depth)
        next(chunk)
        active.append(chunk)
    while active:
        active = [chunk for chunk in active if next(chunk, "end") != "end"]
    for row in range(rows):
        here = jnp.where((row & ((1 << short[0]) - 1)) == 0, 1.0, 0.0)
        out_ref[row * depth : (row + 1) * depth, :] = here * held * gathered[row * depth : (row + 1) * depth, :]


def body(values, levels, coefficients):
    grid_data = values[0]
    level_row = levels[0]
    local_rows = grid_data.shape[0]
    extents = tuple(grid_data.shape[1:])
    groups, members = lax.axis_size("grid"), lax.axis_size("dom")
    lanes = extents[-1]
    depth = int(np.prod(extents[:-1]))

    tops = [local_rows * members] + list(extents)
    ones = [np.ones((points, points)) for points in extents[1:4]]
    inner = []
    for at, points in enumerate(extents[1:4]):
        for table in projection_tables(points):
            factors = ones[:at] + [table] + ones[at + 1 :]
            inner.append(np.kron(np.kron(factors[0], factors[1]), factors[2]))
    inner = jnp.asarray(np.stack(inner), jnp.bfloat16)
    lane = jnp.asarray(np.stack(projection_tables(lanes)).transpose(0, 2, 1), jnp.bfloat16)

    steps = groups.bit_length() - 1
    vmem = pl.BlockSpec(memory_space=pltpu.VMEM)
    smem = pl.BlockSpec(memory_space=pltpu.SMEM)
    combined = pl.pallas_call(
        functools.partial(kernel, groups, members, tops),
        out_shape=jax.ShapeDtypeStruct((local_rows * depth, lanes), jnp.float32),
        in_specs=[vmem, smem, smem, vmem, vmem],
        out_specs=vmem,
        scratch_shapes=[
            pltpu.VMEM((depth, lanes), jnp.float32),
            pltpu.VMEM((local_rows + 1, depth, lanes), jnp.float32),
            pltpu.VMEM((local_rows * depth, lanes), jnp.float32),
            pltpu.VMEM((local_rows * depth, lanes), jnp.float32),
            pltpu.VMEM((local_rows * depth, lanes), jnp.float32),
            pltpu.SemaphoreType.DMA((local_rows, 2 * steps)),
            pltpu.SemaphoreType.DMA((local_rows, 2 * steps)),
            pltpu.SemaphoreType.DMA,
            pltpu.SemaphoreType.DMA,
        ],
        compiler_params=pltpu.CompilerParams(
            collective_id=0, has_side_effects=True, vmem_limit_bytes=40 * 1024 * 1024
        ),
    )(grid_data.reshape(local_rows, depth, lanes), levels, coefficients, inner, lane)
    return combined.reshape(grid_data.shape)[None]


def solution(mesh):
    in_specs = (P("grid", "dom", None, None, None, None, None), P("grid", None), P("grid"))
    out_specs = P("grid", "dom", None, None, None, None, None)
    return jax.shard_map(body, mesh=mesh, in_specs=in_specs, out_specs=out_specs, check_vma=False)
```

```python
import functools

import jax
import jax.numpy as jnp
import numpy as np
from jax import lax
from jax.experimental import pallas as pl
from jax.experimental.pallas import tpu as pltpu
from jax.sharding import PartitionSpec as P

MESH = pl.DeviceIdType.MESH


def coarse_position(numerator, level_now):
    while numerator > 0 and numerator % 2 == 0:
        numerator = numerator // 2
        level_now = level_now - 1
    if numerator == 0:
        return 0
    return (1 << level_now - 1) + (numerator - 1) // 2


def parent_positions(position):
    level_now = position.bit_length()
    span_size = 1 << level_now - 1
    offset = position - span_size
    return [
        coarse_position(offset % span_size, level_now - 1),
        coarse_position((offset + 1) % span_size, level_now - 1),
    ]


def hier_table(points):
    matrix = np.eye(points)
    for position in range(1, points):
        for parent in parent_positions(position):
            matrix[position, parent] -= 0.5
    return matrix


def dehier_table(points):
    matrix = np.zeros((points, points))
    matrix[0, 0] = 1.0
    for position in range(1, points):
        row_now = np.zeros(points)
        row_now[position] = 1.0
        for parent in parent_positions(position):
            row_now = row_now + 0.5 * matrix[parent]
        matrix[position] = row_now
    return matrix


def local_hier(points):
    matrix = np.zeros((points, points + 1))
    matrix[0, 0] = 1.0
    for point in range(1, points):
        stride = point & -point
        matrix[point, point] = 1.0
        matrix[point, point - stride] -= 0.5
        matrix[point, point + stride] -= 0.5
    return matrix


def local_dehier(points):
    matrix = np.zeros((points + 1, points + 1))
    matrix[0, 0] = 1.0
    matrix[points, points] = 1.0
    stride = points // 2
    while stride >= 1:
        for point in range(stride, points, 2 * stride):
            row_now = np.zeros(points + 1)
            row_now[point] = 1.0
            matrix[point] = row_now + 0.5 * (matrix[point - stride] + matrix[point + stride])
        stride = stride // 2
    return matrix[:points]


SHORTFALLS = 3


def projection_tables(points):
    top = points.bit_length() - 1
    hier, dehier = hier_table(points), dehier_table(points)
    return [
        dehier @ np.diag((np.arange(points) < (1 << max(top - s, 0))).astype(np.float64)) @ hier
        for s in range(SHORTFALLS)
    ]


def row_tables(points):
    last = np.zeros((1, points + 1))
    last[0, points] = 1.0
    hier = np.concatenate([local_hier(points), last])
    result = []
    for s in range(SHORTFALLS):
        held = (np.arange(points + 1) % (1 << s) == 0).astype(np.float64)
        held[points] = 1.0
        result.append(local_dehier(points) @ np.diag(held) @ hier)
    return np.stack(result)


def split_dot(data, right=None, left=None):
    high = data.astype(jnp.bfloat16)
    low = (data - high.astype(jnp.float32)).astype(jnp.bfloat16)
    both = jnp.concatenate([high, low], axis=1)
    if right is not None:
        return jnp.dot(both, jnp.concatenate([right, right], axis=0), preferred_element_type=jnp.float32)
    result = jnp.dot(left, both, preferred_element_type=jnp.float32)
    return result[:, : data.shape[1]] + result[:, data.shape[1] :]


def pick(tables, short):
    return [
        [jnp.where(short == 0, float(tables[0][i][j]),
                   jnp.where(short == 1, float(tables[1][i][j]), float(tables[2][i][j])))
         for j in range(len(tables[0][0]))]
        for i in range(len(tables[0]))
    ]


def kernel(groups, members, tops, v_ref, level_ref, weight_ref, inner_ref, lane_ref, out_ref,
           follow, part, acc, recv, gathered, send_sem, recv_sem, z_send, z_recv):
    rows, depth, lanes = v_ref.shape
    steps = groups.bit_length() - 1
    me = lax.axis_index("grid")
    dom = lax.axis_index("dom")
    core = lax.rem(me, 2)
    before = lax.rem(dom + members - 1, members)
    after = lax.rem(dom + 1, members)

    bits, partners = [], []
    for step in range(steps):
        up = 1 << step
        down = 1 << (steps - step) if step else 1
        bit_up = lax.rem(me // up, 2)
        bit_down = lax.rem(me // down, 2)
        bit = bit_up + core * (bit_down - bit_up)
        stride = up + core * (down - up)
        bits.append(bit)
        partners.append(me + (1 - 2 * bit) * stride)

    short = [
        jnp.clip(top.bit_length() - 1 - level_ref[0, k], 0, SHORTFALLS - 1) for k, top in enumerate(tops)
    ]

    barrier = pltpu.get_barrier_semaphore()
    for partner in partners:
        pl.semaphore_signal(barrier, inc=1, device_id={"grid": partner}, device_id_type=MESH)
    for near in (before, after):
        pl.semaphore_signal(barrier, inc=1, device_id={"dom": near}, device_id_type=MESH)
    pl.semaphore_wait(barrier, steps + 2)

    shift = pltpu.make_async_remote_copy(
        src_ref=v_ref.at[0], dst_ref=follow, send_sem=z_send, recv_sem=z_recv,
        device_id={"dom": before}, device_id_type=MESH,
    )
    shift.start()

    outer = tops[1]
    span = depth // outer
    outer_at = pick(projection_tables(outer), short[1])
    row_at = pick(row_tables(rows), short[0])
    weight = weight_ref[0].astype(jnp.float32)
    row_at = [[weight * entry for entry in line] for line in row_at]
    inner = inner_ref[short[2]] * inner_ref[SHORTFALLS + short[3]] * inner_ref[2 * SHORTFALLS + short[4]]
    lane = lane_ref[short[5]]

    def project(data):
        blocks = [split_dot(data[i * span : (i + 1) * span], left=inner) for i in range(outer)]
        mixed = []
        for i in range(outer):
            total = outer_at[i][0] * blocks[0]
            for j in range(1, outer):
                total = total + outer_at[i][j] * blocks[j]
            mixed.append(total)
        return split_dot(jnp.concatenate(mixed, axis=0), right=lane)

    def reduce_chunk(index, start, size):
        low, now = start, size
        lows = [low]
        taken = start
        for step in range(steps):
            half = now // 2
            keep = pl.multiple_of(low + bits[step] * half, 8)
            give = pl.multiple_of(low + (1 - bits[step]) * half, 8)
            copy = pltpu.make_async_remote_copy(
                src_ref=acc.at[pl.ds(give, half)], dst_ref=recv.at[pl.ds(taken, half)],
                send_sem=send_sem.at[index, step], recv_sem=recv_sem.at[index, step],
                device_id={"grid": partners[step]}, device_id_type=MESH,
            )
            copy.start()
            yield
            copy.wait()
            total = acc[pl.ds(keep, half), :] + recv[taken : taken + half, :]
            if step == steps - 1:
                gathered[pl.ds(keep, half), :] = total
            else:
                acc[pl.ds(keep, half), :] = total
            taken += half
            low, now = keep, half
            lows.append(low)
        for step in range(steps - 1, -1, -1):
            mine = gathered.at[pl.ds(lows[step + 1], now)]
            copy = pltpu.make_async_remote_copy(
                src_ref=mine, dst_ref=mine,
                send_sem=send_sem.at[index, 2 * steps - 1 - step],
                recv_sem=recv_sem.at[index, 2 * steps - 1 - step],
                device_id={"grid": partners[step]}, device_id_type=MESH,
            )
            copy.start()
            yield
            copy.wait()
            now *= 2

    place = lax.broadcasted_iota(jnp.int32, (depth, lanes), 0)
    inside = lax.broadcasted_iota(jnp.int32, (depth, lanes), 1) < (lanes >> short[5])
    below = depth
    for k in range(1, 5):
        below //= tops[k]
        inside &= ((place // below) % tops[k]) < (tops[k] >> short[k])
    held = inside.astype(jnp.float32)

    first = project(v_ref[0])
    part[0] = first
    acc[0:depth, :] = row_at[0][0] * first
    head = reduce_chunk(0, 0, depth)
    next(head)
    for row in range(1, rows):
        part[row] = project(v_ref[row])
    next(head)
    shift.wait()
    next(head)
    part[rows] = project(follow[...])
    active = [head]
    for row in range(1, rows):
        total = row_at[row][0] * part[0]
        for source in range(1, rows + 1):
            total = total + row_at[row][source] * part[source]
        acc[row * depth : (row + 1) * depth, :] = total
        chunk = reduce_chunk(row, row * depth, depth)
        next(chunk)
        active.append(chunk)
    while active:
        active = [chunk for chunk in active if next(chunk, "end") != "end"]
    for row in range(rows):
        here = jnp.where((row & ((1 << short[0]) - 1)) == 0, 1.0, 0.0)
        out_ref[row * depth : (row + 1) * depth, :] = here * held * gathered[row * depth : (row + 1) * depth, :]


def body(values, levels, coefficients):
    grid_data = values[0]
    level_row = levels[0]
    local_rows = grid_data.shape[0]
    extents = tuple(grid_data.shape[1:])
    groups, members = lax.axis_size("grid"), lax.axis_size("dom")
    lanes = extents[-1]
    depth = int(np.prod(extents[:-1]))

    tops = [local_rows * members] + list(extents)
    ones = [np.ones((points, points)) for points in extents[1:4]]
    inner = []
    for at, points in enumerate(extents[1:4]):
        for table in projection_tables(points):
            factors = ones[:at] + [table] + ones[at + 1 :]
            inner.append(np.kron(np.kron(factors[0], factors[1]), factors[2]))
    inner = jnp.asarray(np.stack(inner), jnp.bfloat16)
    lane = jnp.asarray(np.stack(projection_tables(lanes)).transpose(0, 2, 1), jnp.bfloat16)

    steps = groups.bit_length() - 1
    vmem = pl.BlockSpec(memory_space=pltpu.VMEM)
    smem = pl.BlockSpec(memory_space=pltpu.SMEM)
    combined = pl.pallas_call(
        functools.partial(kernel, groups, members, tops),
        out_shape=jax.ShapeDtypeStruct((local_rows * depth, lanes), jnp.float32),
        in_specs=[vmem, smem, smem, vmem, vmem],
        out_specs=vmem,
        scratch_shapes=[
            pltpu.VMEM((depth, lanes), jnp.float32),
            pltpu.VMEM((local_rows + 1, depth, lanes), jnp.float32),
            pltpu.VMEM((local_rows * depth, lanes), jnp.float32),
            pltpu.VMEM((local_rows * depth, lanes), jnp.float32),
            pltpu.VMEM((local_rows * depth, lanes), jnp.float32),
            pltpu.SemaphoreType.DMA((local_rows, 2 * steps)),
            pltpu.SemaphoreType.DMA((local_rows, 2 * steps)),
            pltpu.SemaphoreType.DMA,
            pltpu.SemaphoreType.DMA,
        ],
        compiler_params=pltpu.CompilerParams(
            collective_id=0, has_side_effects=True, vmem_limit_bytes=40 * 1024 * 1024
        ),
    )(grid_data.reshape(local_rows, depth, lanes), levels, coefficients, inner, lane)
    return combined.reshape(grid_data.shape)[None]


def solution(mesh):
    in_specs = (P("grid", "dom", None, None, None, None, None), P("grid", None), P("grid"))
    out_specs = P("grid", "dom", None, None, None, None, None)
    return jax.shard_map(body, mesh=mesh, in_specs=in_specs, out_specs=out_specs, check_vma=False)
```
